32 devices in a mesh: ctx: 4 (over y, core), ch: 2 (over x), dp: 4 (over z).
Axes of the slice: x: 2, y: 2, z: 4, core: 2. Of those that a mesh axis runs over, the one named last changes fastest.
Arguments:
- features: bfloat16 [8192, 3, 4096], P(('dp', 'ctx'), None, 'ch'), parts along dimension 0, may hold values from -6 to 6
- short_filter: float32 [3, 3, 4096], P(None, None, 'ch'), may hold values from -3.5 to 3.5
- mode_residue: float32 [16, 4096], P(None, 'ch'), may hold values from -0.18 to 0.18
- decay_mix: float32 [16, 4096], P(None, 'ch'), may hold values from 0 to 1
- skip_gain: float32 [4096], P('ch'), may hold values from 0.5 to 1.5
- counter: int32 [8], P('dp'), parts along dimension 0, may hold values from 0 to 1048575
- out_weight: bfloat16 [4096, 4096], P('ch'), may hold values from -0.09375 to 0.09375
Outputs:
- projected: bfloat16 [8192, 4096], P(('dp', 'ctx', 'ch')), parts along dimension 0
The draws below stay inside these ranges and needn't reach their ends.
There are 4 independent parts, one for each index of `dp`. The reference program is written for one: setup_inputs(seed, part) draws one part's arguments, and reference() takes and returns one part's arrays. A program takes and returns all parts, laid end to end along the dimension named above; an argument that names none is the same for every part. Nothing has to cross between parts.
All inputs are finite; a program needn't handle non-finite values.
Results may differ from the reference program's by a relative error of at most 0.012.
Values may be sent and summed in bfloat16 or wider, within the bound.
A program may use at most 256 MiB of HBM per device.

```python
import math
import jax
import jax.numpy as jnp
from jax import lax

DW = 4096
DO = 4096
ORD = 16
SHORT = 3
TOKENS = 2048


def draw_decay_mix(key, part):
    values = jax.random.uniform(key, (ORD, DW), jnp.float32)
    return values


def shard_levels(own_key, extent, cuts, low, high):
    def one(position, blocks):
        heights = jax.random.uniform(jax.random.fold_in(jax.random.fold_in(own_key, 6), position), (blocks,), jnp.float32, low / len(cuts), high / len(cuts))
        return jnp.repeat(jnp.exp(heights), extent[position] // blocks).reshape((-1,) + (1,) * (len(extent) - position - 1))

    level = one(*cuts[0])
    for cut in cuts[1:]:
        level = level * one(*cut)
    return level


def centred(stream_key, shape, spread, most, split=(), kind=jnp.bfloat16):
    result = spread * jax.random.normal(stream_key, shape, jnp.float32)
    if split:
        result = result * shard_levels(stream_key, shape, split, -0.22, 0.18)
    return jnp.clip(result, -most, most).astype(kind)


def setup_inputs(seed: int = 0, part: int = 0) -> dict:
    keys = jax.random.split(jax.random.key(seed), 8)
    part_keys = jax.random.split(jax.random.fold_in(keys[7], part), 8)
    return {
        "features": centred(part_keys[0], (TOKENS, 3, DW), 1.0, 6.0, ((0, 4), (2, 2))),
        "short_filter": centred(keys[1], (3, SHORT, DW), SHORT ** -0.5, 3.5, ((2, 2),), jnp.float32),
        "mode_residue": centred(keys[2], (ORD, DW), 0.03, 0.18, ((1, 2),), jnp.float32),
        "decay_mix": draw_decay_mix(jax.random.fold_in(keys[7], 71), part),
        "skip_gain": jnp.clip(0.5 + 1.0 * jax.random.uniform(keys[4], (DW,), jnp.float32) ** shard_levels(keys[4], (DW,), ((0, 2),), -0.2, 0.2), 0.5, 1.5),
        "counter": jax.random.randint(part_keys[5], (2,), 0, 1048576).astype(jnp.int32),
        "out_weight": centred(keys[6], (DW, DO), DW ** -0.5, 0.09375, ((0, 2),)),
    }


keep_scale = 8.0 / 7.0


def keep_mask(hash_base, positions, channels):
    bits = hash_base + positions[:, None] * jnp.int32(-1640531535) + channels[None, :] * jnp.int32(-2048144777)
    bits = bits ^ lax.shift_right_logical(bits, jnp.full_like(bits, 16))
    bits = bits * jnp.int32(2146121005)
    bits = bits ^ lax.shift_right_logical(bits, jnp.full_like(bits, 15))
    bits = bits * jnp.int32(-2073254261)
    bits = bits ^ lax.shift_right_logical(bits, jnp.full_like(bits, 16))
    return lax.shift_right_logical(bits, jnp.full_like(bits, 29)) != 0


def rates_of(mix, length):
    return jnp.exp(-((1.0 - mix) * math.log(length) + mix * math.log(30.0)))


def build_filter(residue, mix, length):
    rates = rates_of(mix, length)
    times = jnp.arange(length, dtype=jnp.int32).astype(jnp.float32)

    def add_mode(order_index, total):
        return total + residue[order_index][None, :] * jnp.exp(-rates[order_index][None, :] * times[:, None])

    return lax.fori_loop(0, residue.shape[0], add_mode, jnp.zeros((length, residue.shape[1]), jnp.float32))


def reference(features, short_filter, mode_residue, decay_mix, skip_gain, counter, out_weight):
    padded = jnp.concatenate([jnp.zeros((SHORT - 1, 3, DW), jnp.bfloat16), features], axis=0).astype(jnp.float32)
    filtered = jnp.zeros((TOKENS, 3, DW), jnp.float32)
    for lag in range(SHORT):
        filtered = filtered + short_filter[:, lag, :][None] * padded[SHORT - 1 - lag:SHORT - 1 - lag + TOKENS]
    query = filtered[:, 0]
    keyed = filtered[:, 1]
    valued = filtered[:, 2]
    positions = counter[1] + jnp.arange(TOKENS, dtype=jnp.int32)
    channels = jnp.arange(DW, dtype=jnp.int32)
    gated = jnp.where(keep_mask(counter[0], positions, channels), keyed * valued * keep_scale, 0.0).astype(jnp.bfloat16)
    gated_wide = gated.astype(jnp.float32)
    long_filter = build_filter(mode_residue, decay_mix, TOKENS)
    total_len = 2 * TOKENS
    spectrum = jnp.fft.rfft(gated_wide, n=total_len, axis=0) * jnp.fft.rfft(long_filter, n=total_len, axis=0)
    convolved = jnp.fft.irfft(spectrum, n=total_len, axis=0)[:TOKENS]
    long_out = convolved + skip_gain[None, :] * gated_wide
    mixed = (query * long_out).astype(jnp.bfloat16)
    return jnp.dot(mixed, out_weight, preferred_element_type=jnp.float32).astype(jnp.bfloat16)
```

```python
import functools
import math

import jax
import jax.numpy as jnp
from jax import lax
from jax.experimental import pallas as pl
from jax.experimental.pallas import tpu as pltpu
from jax.sharding import PartitionSpec as P

SHORT = 3
LANES = 128
CHUNKS = 8
HALO = 8
keep_scale = 8.0 / 7.0
POS_MULT = -1640531535
CHAN_MULT = -2048144777


def passed_along(value, axis, steps):
    count = lax.axis_size(axis)
    return lax.ppermute(value, axis, [(source, source + steps) for source in range(count - steps)])


def rates_of(mix, length):
    return jnp.exp(-((1.0 - mix) * math.log(length) + mix * math.log(30.0)))


def tapped(before, block, taps):
    rows = block.shape[0]
    joined = jnp.concatenate([before, block], axis=0)
    total = taps[0:1] * block
    for lag in range(1, SHORT):
        total = total + taps[lag : lag + 1] * joined[HALO - lag : HALO - lag + rows]
    return total


def keep_mask(bits):
    bits = bits ^ lax.shift_right_logical(bits, jnp.full_like(bits, 16))
    bits = bits * jnp.int32(2146121005)
    bits = bits ^ lax.shift_right_logical(bits, jnp.full_like(bits, 15))
    bits = bits * jnp.int32(-2073254261)
    bits = bits ^ lax.shift_right_logical(bits, jnp.full_like(bits, 16))
    return lax.shift_right_logical(bits, jnp.full_like(bits, 29)) != 0


def spread(table, row, lanes):
    return jnp.broadcast_to(table[row : row + 1, lanes], (CHUNKS, LANES))


def gate_kernel(length, step, unroll, base_ref, feat_ref, edge_ref, taps_ref, mix_ref,
                gated_ref, start_ref, end_ref, wide, sums):
    rows, width = gated_ref.shape
    groups = width // LANES
    modes = mix_ref.shape[0]
    run_len = rows // CHUNKS
    first_channel = pl.program_id(0) * width
    base = base_ref[0] + first_channel * jnp.int32(CHAN_MULT)
    shape = (step, width)
    offsets = (
        lax.broadcasted_iota(jnp.int32, shape, 0) * jnp.int32(POS_MULT)
        + lax.broadcasted_iota(jnp.int32, shape, 1) * jnp.int32(CHAN_MULT)
    )
    key_taps, value_taps = taps_ref[1], taps_ref[2]

    def gate(index, before):
        at = pl.ds(pl.multiple_of(index * step, step), step)
        key_in = feat_ref[1, at, :].astype(jnp.float32)
        value_in = feat_ref[2, at, :].astype(jnp.float32)
        keyed = tapped(before[0], key_in, key_taps)
        valued = tapped(before[1], value_in, value_taps)
        bits = offsets + (base + index * step * jnp.int32(POS_MULT))
        gated = jnp.where(keep_mask(bits), keyed * valued * keep_scale, 0.0).astype(jnp.bfloat16)
        gated_ref[at, :] = gated
        full = gated.astype(jnp.float32)
        for group in range(groups):
            wide[group, at, :] = full[:, group * LANES : (group + 1) * LANES]
        return (key_in[step - HALO :], value_in[step - HALO :])

    lax.fori_loop(
        0, rows // step, gate,
        (edge_ref[1].astype(jnp.float32), edge_ref[2].astype(jnp.float32)),
    )

    rate = rates_of(mix_ref[...], length)
    decay = jnp.exp(-rate)
    decay_run = jnp.exp(-rate * run_len)
    for group in range(groups):
        lanes = slice(group * LANES, (group + 1) * LANES)
        factors = [spread(decay, mode, lanes) for mode in range(modes)]

        def advance(block, states):
            for inner in range(unroll):
                x = wide[group, pl.ds(block * unroll + inner, CHUNKS, stride=run_len), :]
                states = tuple(f * s + x for f, s in zip(factors, states))
            return states

        states = lax.fori_loop(
            0, run_len // unroll, advance,
            tuple(jnp.zeros((CHUNKS, LANES), jnp.float32) for _ in range(modes)),
        )
        for mode in range(modes):
            sums[pl.ds(mode * CHUNKS, CHUNKS), :] = states[mode]
        running = jnp.zeros((modes, LANES), jnp.float32)
        for chunk in range(CHUNKS):
            start_ref[group, pl.ds(chunk * modes, modes), :] = running
            running = decay_run[:, lanes] * running + sums[pl.ds(chunk, modes, stride=CHUNKS), :]
        end_ref[:, lanes] = running


def conv_kernel(length, step, unroll, feat_ref, edge_ref, taps_ref, residue_ref, mix_ref,
                skip_ref, gated_ref, start_ref, *rest):
    end_refs, (mixed_ref, wide, inits) = rest[:-3], rest[-3:]
    rows, width = gated_ref.shape
    groups = width // LANES
    modes = mix_ref.shape[0]
    run_len = rows // CHUNKS

    def widen(index, carry):
        at = pl.ds(pl.multiple_of(index * step, step), step)
        full = gated_ref[at, :].astype(jnp.float32)
        for group in range(groups):
            wide[group, at, :] = full[:, group * LANES : (group + 1) * LANES]
        return carry

    lax.fori_loop(0, rows // step, widen, 0)
    rate = rates_of(mix_ref[...], length)
    decay = jnp.exp(-rate)
    residue = residue_ref[...]
    entry = jnp.zeros_like(rate)
    for back, end_ref in enumerate(end_refs):
        entry = entry + jnp.exp(-rate * (rows * back)) * end_ref[...]
    for group in range(groups):
        lanes = slice(group * LANES, (group + 1) * LANES)
        for chunk in range(CHUNKS):
            at = pl.ds(chunk * modes, modes)
            reach = jnp.exp(-rate[:, lanes] * (run_len * chunk))
            inits[at, :] = residue[:, lanes] * (start_ref[group, at, :] + reach * entry[:, lanes])
        factors = [spread(decay, mode, lanes) for mode in range(modes)]
        gains = [spread(residue, mode, lanes) for mode in range(modes)]

        def advance(block, states):
            for inner in range(unroll):
                at = pl.ds(block * unroll + inner, CHUNKS, stride=run_len)
                x = wide[group, at, :]
                states = tuple(f * s + k * x for f, s, k in zip(factors, states, gains))
                parts = list(states)
                while len(parts) > 1:
                    odd = [parts[-1]] if len(parts) % 2 else []
                    parts = [p + q for p, q in zip(parts[0::2], parts[1::2])] + odd
                wide[group, at, :] = parts[0]
            return states

        lax.fori_loop(
            0, run_len // unroll, advance,
            tuple(inits[pl.ds(mode, CHUNKS, stride=modes), :] for mode in range(modes)),
        )

    taps = taps_ref[0]
    skip = skip_ref[...]

    def mix(index, before):
        at = pl.ds(pl.multiple_of(index * step, step), step)
        query_in = feat_ref[0, at, :].astype(jnp.float32)
        query = tapped(before, query_in, taps)
        convolved = jnp.concatenate([wide[group, at, :] for group in range(groups)], axis=1)
        long_out = convolved + skip * gated_ref[at, :].astype(jnp.float32)
        mixed_ref[at, :] = (query * long_out).astype(jnp.bfloat16)
        return query_in[step - HALO :]

    lax.fori_loop(0, rows // step, mix, edge_ref[0].astype(jnp.float32))


def body(features, short_filter, mode_residue, decay_mix, skip_gain, counter, out_weight):
    rows, kinds, width = features.shape
    modes = mode_residue.shape[0]
    ctx_count = lax.axis_size("ctx")
    ch_count = lax.axis_size("ch")
    length = rows * ctx_count
    run_len = rows // CHUNKS
    tile = 2 * LANES if width % (2 * LANES) == 0 else LANES
    groups = tile // LANES
    step = min(64, rows)
    unroll = min(8, run_len)
    grid = (width // tile,)

    edge = passed_along(features[rows - HALO :], "ctx", 1).transpose(1, 0, 2)
    planes = features.transpose(1, 0, 2)
    first = counter[1] + lax.axis_index("ctx") * rows
    base = (
        counter[0] + first * jnp.int32(POS_MULT)
        + lax.axis_index("ch") * width * jnp.int32(CHAN_MULT)
    )[None]

    plane_block = pl.BlockSpec((kinds, rows, tile), lambda i: (0, 0, i))
    query_block = pl.BlockSpec((1, rows, tile), lambda i: (0, 0, i))
    edge_block = pl.BlockSpec((kinds, HALO, tile), lambda i: (0, 0, i))
    taps_block = pl.BlockSpec((kinds, SHORT, tile), lambda i: (0, 0, i))
    mode_block = pl.BlockSpec((modes, tile), lambda i: (0, i))
    row_block = pl.BlockSpec((rows, tile), lambda i: (0, i))
    start_block = pl.BlockSpec((groups, modes * CHUNKS, LANES), lambda i: (i, 0, 0))
    skip_block = pl.BlockSpec((1, tile), lambda i: (0, i))
    params = pltpu.CompilerParams(vmem_limit_bytes=32 * 1024 * 1024)

    gated, starts, ends = pl.pallas_call(
        functools.partial(gate_kernel, length, step, unroll),
        grid=grid,
        in_specs=[
            pl.BlockSpec(memory_space=pltpu.SMEM), plane_block, edge_block, taps_block, mode_block,
        ],
        out_specs=[row_block, start_block, mode_block],
        out_shape=[
            jax.ShapeDtypeStruct((rows, width), jnp.bfloat16),
            jax.ShapeDtypeStruct((width // LANES, modes * CHUNKS, LANES), jnp.float32),
            jax.ShapeDtypeStruct((modes, width), jnp.float32),
        ],
        scratch_shapes=[
            pltpu.VMEM((groups, rows, LANES), jnp.float32),
            pltpu.VMEM((modes * CHUNKS, LANES), jnp.float32),
        ],
        compiler_params=params,
        name="gate",
    )(base, planes, edge, short_filter, decay_mix)

    arrived = [passed_along(ends, "ctx", steps) for steps in range(1, ctx_count)]

    mixed = pl.pallas_call(
        functools.partial(conv_kernel, length, step, unroll),
        grid=grid,
        in_specs=[
            query_block, edge_block, taps_block, mode_block, mode_block, skip_block, row_block,
            start_block,
        ] + [mode_block] * len(arrived),
        out_specs=row_block,
        out_shape=jax.ShapeDtypeStruct((rows, width), jnp.bfloat16),
        scratch_shapes=[
            pltpu.VMEM((groups, rows, LANES), jnp.float32),
            pltpu.VMEM((modes * CHUNKS, LANES), jnp.float32),
        ],
        compiler_params=params,
        name="conv",
    )(planes, edge, short_filter, mode_residue, decay_mix, skip_gain[None], gated, starts, *arrived)

    if ch_count != 2:
        partial = jnp.dot(mixed, out_weight, preferred_element_type=jnp.float32)
        return lax.psum_scatter(
            partial.astype(jnp.bfloat16), "ch", scatter_dimension=0, tiled=True
        )
    half = rows // 2
    me = lax.axis_index("ch")
    theirs = lax.dynamic_slice_in_dim(mixed, (1 - me) * half, half, 0)
    ours = lax.dynamic_slice_in_dim(mixed, me * half, half, 0)
    features_out = out_weight.shape[1]
    pieces = 4
    piece = features_out // pieces
    received = []
    for index in range(pieces):
        part = jnp.dot(
            theirs, out_weight[:, index * piece : (index + 1) * piece],
            preferred_element_type=jnp.float32,
        ).astype(jnp.bfloat16)
        received.append(lax.ppermute(part, "ch", [(0, 1), (1, 0)]))
    own = jnp.dot(ours, out_weight, preferred_element_type=jnp.float32)
    got = jnp.concatenate(received, axis=1)
    return (own + got.astype(jnp.float32)).astype(jnp.bfloat16)


def solution(mesh):
    placed = (
        P(("dp", "ctx"), None, "ch"),
        P(None, None, "ch"),
        P(None, "ch"),
        P(None, "ch"),
        P("ch"),
        P("dp"),
        P("ch", None),
    )
    return jax.shard_map(
        body, mesh=mesh, in_specs=placed, out_specs=P(("dp", "ctx", "ch"), None), check_vma=False
    )
```

```python
import functools
import math

import jax
import jax.numpy as jnp
from jax import lax
from jax.experimental import pallas as pl
from jax.experimental.pallas import tpu as pltpu
from jax.sharding import PartitionSpec as P

SHORT = 3
LANES = 128
CHUNKS = 8
HALO = 8
keep_scale = 8.0 / 7.0
POS_MULT = -1640531535
CHAN_MULT = -2048144777


def passed_along(value, axis, steps):
    count = lax.axis_size(axis)
    return lax.ppermute(value, axis, [(source, source + steps) for source in range(count - steps)])


def rates_of(mix, length):
    return jnp.exp(-((1.0 - mix) * math.log(length) + mix * math.log(30.0)))


def tapped(before, block, taps):
    rows = block.shape[0]
    joined = jnp.concatenate([before, block], axis=0)
    total = taps[0:1] * block
    for lag in range(1, SHORT):
        total = total + taps[lag : lag + 1] * joined[HALO - lag : HALO - lag + rows]
    return total


def keep_mask(bits):
    bits = bits ^ lax.shift_right_logical(bits, jnp.full_like(bits, 16))
    bits = bits * jnp.int32(2146121005)
    bits = bits ^ lax.shift_right_logical(bits, jnp.full_like(bits, 15))
    bits = bits * jnp.int32(-2073254261)
    bits = bits ^ lax.shift_right_logical(bits, jnp.full_like(bits, 16))
    return lax.shift_right_logical(bits, jnp.full_like(bits, 29)) != 0


def spread(table, row, lanes):
    return jnp.broadcast_to(table[row : row + 1, lanes], (CHUNKS, LANES))


def gate_kernel(length, step, unroll, base_ref, feat_ref, edge_ref, taps_ref, mix_ref,
                gated_ref, start_ref, end_ref, wide, sums):
    rows, width = gated_ref.shape
    groups = width // LANES
    modes = mix_ref.shape[0]
    parts = start_ref.shape[1] // (modes * CHUNKS)
    run_len = rows // (CHUNKS * parts)
    first_channel = pl.program_id(0) * width
    base = base_ref[0] + first_channel * jnp.int32(CHAN_MULT)
    shape = (step, width)
    offsets = (
        lax.broadcasted_iota(jnp.int32, shape, 0) * jnp.int32(POS_MULT)
        + lax.broadcasted_iota(jnp.int32, shape, 1) * jnp.int32(CHAN_MULT)
    )
    key_taps, value_taps = taps_ref[1], taps_ref[2]

    def gate(index, before):
        at = pl.ds(pl.multiple_of(index * step, step), step)
        key_in = feat_ref[1, at, :].astype(jnp.float32)
        value_in = feat_ref[2, at, :].astype(jnp.float32)
        keyed = tapped(before[0], key_in, key_taps)
        valued = tapped(before[1], value_in, value_taps)
        bits = offsets + (base + index * step * jnp.int32(POS_MULT))
        gated = jnp.where(keep_mask(bits), keyed * valued * keep_scale, 0.0).astype(jnp.bfloat16)
        gated_ref[at, :] = gated
        full = gated.astype(jnp.float32)
        for group in range(groups):
            wide[group, at, :] = full[:, group * LANES : (group + 1) * LANES]
        return (key_in[step - HALO :], value_in[step - HALO :])

    lax.fori_loop(
        0, rows // step, gate,
        (edge_ref[1].astype(jnp.float32), edge_ref[2].astype(jnp.float32)),
    )

    rate = rates_of(mix_ref[...], length)
    decay = jnp.exp(-rate)
    decay_run = jnp.exp(-rate * run_len)
    for group in range(groups):
        lanes = slice(group * LANES, (group + 1) * LANES)
        factors = [spread(decay, mode, lanes) for mode in range(modes)]

        running = jnp.zeros((modes, LANES), jnp.float32)
        for part in range(parts):

            def advance(block, states):
                for inner in range(unroll):
                    first = part * CHUNKS * run_len + block * unroll + inner
                    x = wide[group, pl.ds(first, CHUNKS, stride=run_len), :]
                    states = tuple(f * s + x for f, s in zip(factors, states))
                return states

            states = lax.fori_loop(
                0, run_len // unroll, advance,
                tuple(jnp.zeros((CHUNKS, LANES), jnp.float32) for _ in range(modes)),
            )
            for mode in range(modes):
                sums[part, pl.ds(mode * CHUNKS, CHUNKS), :] = states[mode]
            for chunk in range(CHUNKS):
                start_ref[group, pl.ds((part * CHUNKS + chunk) * modes, modes), :] = running
                running = (
                    decay_run[:, lanes] * running
                    + sums[part, pl.ds(chunk, modes, stride=CHUNKS), :]
                )
        end_ref[:, lanes] = running


def conv_kernel(length, device_rows, lags, step, unroll, part_ref, feat_ref, prior_ref, edge_ref, taps_ref,
                residue_ref, mix_ref, skip_ref, gated_ref, start_ref, *rest):
    (mixed_ref, wide, inits), end_refs = rest[-3:], rest[:lags]
    rows, width = gated_ref.shape
    groups = width // LANES
    modes = mix_ref.shape[0]
    run_len = rows // CHUNKS
    part = part_ref[0]

    def widen(index, carry):
        at = pl.ds(pl.multiple_of(index * step, step), step)
        full = gated_ref[at, :].astype(jnp.float32)
        for group in range(groups):
            wide[group, at, :] = full[:, group * LANES : (group + 1) * LANES]
        return carry

    lax.fori_loop(0, rows // step, widen, 0)
    rate = rates_of(mix_ref[...], length)
    decay = jnp.exp(-rate)
    residue = residue_ref[...]
    entry = jnp.zeros_like(rate)
    for back, end_ref in enumerate(end_refs):
        entry = entry + jnp.exp(-rate * (device_rows * back)) * end_ref[...]
    for group in range(groups):
        lanes = slice(group * LANES, (group + 1) * LANES)
        for chunk in range(CHUNKS):
            at = pl.ds(chunk * modes, modes)
            reach = jnp.exp(-rate[:, lanes] * (part * rows + run_len * chunk).astype(jnp.float32))
            inits[at, :] = residue[:, lanes] * (start_ref[group, at, :] + reach * entry[:, lanes])
        factors = [spread(decay, mode, lanes) for mode in range(modes)]
        gains = [spread(residue, mode, lanes) for mode in range(modes)]

        def advance(block, states):
            for inner in range(unroll):
                at = pl.ds(block * unroll + inner, CHUNKS, stride=run_len)
                x = wide[group, at, :]
                states = tuple(f * s + k * x for f, s, k in zip(factors, states, gains))
                parts = list(states)
                while len(parts) > 1:
                    odd = [parts[-1]] if len(parts) % 2 else []
                    parts = [p + q for p, q in zip(parts[0::2], parts[1::2])] + odd
                wide[group, at, :] = parts[0]
            return states

        lax.fori_loop(
            0, run_len // unroll, advance,
            tuple(inits[pl.ds(mode, CHUNKS, stride=modes), :] for mode in range(modes)),
        )

    taps = taps_ref[0]
    skip = skip_ref[...]

    def mix(index, before):
        at = pl.ds(pl.multiple_of(index * step, step), step)
        query_in = feat_ref[0, at, :].astype(jnp.float32)
        query = tapped(before, query_in, taps)
        convolved = jnp.concatenate([wide[group, at, :] for group in range(groups)], axis=1)
        long_out = convolved + skip * gated_ref[at, :].astype(jnp.float32)
        mixed_ref[at, :] = (query * long_out).astype(jnp.bfloat16)
        return query_in[step - HALO :]

    before = jnp.where(
        part == 0,
        edge_ref[0].astype(jnp.float32),
        prior_ref[0].astype(jnp.float32)[prior_ref.shape[1] - HALO :],
    )
    lax.fori_loop(0, rows // step, mix, before)


def body(features, short_filter, mode_residue, decay_mix, skip_gain, counter, out_weight):
    rows, kinds, width = features.shape
    modes = mode_residue.shape[0]
    ctx_count = lax.axis_size("ctx")
    ch_count = lax.axis_size("ch")
    length = rows * ctx_count
    half = rows // ch_count
    run_len = half // CHUNKS
    tile = 2 * LANES if width % (2 * LANES) == 0 else LANES
    groups = tile // LANES
    step = min(64, half)
    unroll = min(8, run_len)
    grid = (width // tile,)
    prior = 2 * HALO

    planes = features.transpose(1, 0, 2)
    edge = passed_along(planes[:, rows - HALO :], "ctx", 1)
    first = counter[1] + lax.axis_index("ctx") * rows
    base = (
        counter[0] + first * jnp.int32(POS_MULT)
        + lax.axis_index("ch") * width * jnp.int32(CHAN_MULT)
    )[None]

    params = pltpu.CompilerParams(vmem_limit_bytes=60 * 1024 * 1024)

    gated, starts, ends = pl.pallas_call(
        functools.partial(gate_kernel, length, step, unroll),
        grid=grid,
        in_specs=[
            pl.BlockSpec(memory_space=pltpu.SMEM),
            pl.BlockSpec((kinds, rows, tile), lambda i: (0, 0, i)),
            pl.BlockSpec((kinds, HALO, tile), lambda i: (0, 0, i)),
            pl.BlockSpec((kinds, SHORT, tile), lambda i: (0, 0, i)),
            pl.BlockSpec((modes, tile), lambda i: (0, i)),
        ],
        out_specs=[
            pl.BlockSpec((rows, tile), lambda i: (0, i)),
            pl.BlockSpec((groups, ch_count * modes * CHUNKS, LANES), lambda i: (i, 0, 0)),
            pl.BlockSpec((modes, tile), lambda i: (0, i)),
        ],
        out_shape=[
            jax.ShapeDtypeStruct((rows, width), jnp.bfloat16),
            jax.ShapeDtypeStruct((width // LANES, ch_count * modes * CHUNKS, LANES), jnp.float32),
            jax.ShapeDtypeStruct((modes, width), jnp.float32),
        ],
        scratch_shapes=[
            pltpu.VMEM((groups, rows, LANES), jnp.float32),
            pltpu.VMEM((ch_count, modes * CHUNKS, LANES), jnp.float32),
        ],
        compiler_params=params,
        cost_estimate=pl.CostEstimate(flops=10**10, bytes_accessed=10**7, transcendentals=0),
        name="gate",
    )(base, planes, edge, short_filter, decay_mix)

    arrived = [passed_along(ends, "ctx", steps) for steps in range(1, ctx_count)]
    mode_block = pl.BlockSpec((modes, tile), lambda i, p: (0, i))

    def mixed_part(part, *after):
        return pl.pallas_call(
            functools.partial(conv_kernel, length, rows, len(arrived), step, unroll),
            grid_spec=pltpu.PrefetchScalarGridSpec(
                num_scalar_prefetch=1,
                grid=grid,
                in_specs=[
                    pl.BlockSpec((1, half, tile), lambda i, p: (0, p[0], i)),
                    pl.BlockSpec(
                        (1, prior, tile),
                        lambda i, p: (0, jnp.maximum(p[0] * (half // prior) - 1, 0), i),
                    ),
                    pl.BlockSpec((1, HALO, tile), lambda i, p: (0, 0, i)),
                    pl.BlockSpec((kinds, SHORT, tile), lambda i, p: (0, 0, i)),
                    mode_block,
                    mode_block,
                    pl.BlockSpec((1, tile), lambda i, p: (0, i)),
                    pl.BlockSpec((half, tile), lambda i, p: (p[0], i)),
                    pl.BlockSpec((groups, modes * CHUNKS, LANES), lambda i, p: (i, p[0], 0)),
                ] + [mode_block] * len(arrived) + [pl.BlockSpec(memory_space=pl.ANY)] * len(after),
                out_specs=pl.BlockSpec((half, tile), lambda i, p: (0, i)),
                scratch_shapes=[
                    pltpu.VMEM((groups, half, LANES), jnp.float32),
                    pltpu.VMEM((modes * CHUNKS, LANES), jnp.float32),
                ],
            ),
            out_shape=jax.ShapeDtypeStruct((half, width), jnp.bfloat16),
            compiler_params=params,
            cost_estimate=pl.CostEstimate(flops=8 * 10**9, bytes_accessed=10**7, transcendentals=0),
            name="conv",
        )(
            part[None], planes, planes, edge, short_filter, mode_residue, decay_mix,
            skip_gain[None], gated, starts, *arrived, *after,
        )

    me = lax.axis_index("ch")
    eighth = out_weight.shape[1] // 8
    columns = [slice(low * eighth, high * eighth) for low, high in zip((0, 1, 3, 5, 7), (1, 3, 5, 7, 8))]
    sent = []
    received = []
    for away in range(1, ch_count):
        theirs = mixed_part((me + away) % ch_count)
        arrivals = []
        for cut in columns:
            part = jnp.dot(theirs, out_weight[:, cut], preferred_element_type=jnp.float32)
            theirs, part = lax.optimization_barrier((theirs, part.astype(jnp.bfloat16)))
            route = [(source, (source + away) % ch_count) for source in range(ch_count)]
            arrivals.append(lax.ppermute(part, "ch", route))
        sent.append(part)
        received.append(arrivals)
    ours = mixed_part(me, *sent)
    own = lax.optimization_barrier(
        jnp.dot(ours, out_weight, preferred_element_type=jnp.float32)
    )
    outs = []
    for index, cut in enumerate(columns):
        total = own[:, cut]
        for arrivals in received:
            total = total + arrivals[index].astype(jnp.float32)
        outs.append(total.astype(jnp.bfloat16))
    return jnp.concatenate(outs, axis=1)


def solution(mesh):
    placed = (
        P(("dp", "ctx"), None, "ch"),
        P(None, None, "ch"),
        P(None, "ch"),
        P(None, "ch"),
        P("ch"),
        P("dp"),
        P("ch", None),
    )
    return jax.shard_map(
        body, mesh=mesh, in_specs=placed, out_specs=P(("dp", "ctx", "ch"), None), check_vma=False
    )
```

```python
import functools
import math

import jax
import jax.numpy as jnp
from jax import lax
from jax.experimental import pallas as pl
from jax.experimental.pallas import tpu as pltpu
from jax.sharding import PartitionSpec as P

SHORT = 3
LANES = 128
CHUNKS = 8
HALO = 8
keep_scale = 8.0 / 7.0
POS_MULT = -1640531535
CHAN_MULT = -2048144777


def passed_along(value, axis, steps):
    count = lax.axis_size(axis)
    return lax.ppermute(value, axis, [(source, source + steps) for source in range(count - steps)])


def rates_of(mix, length):
    return jnp.exp(-((1.0 - mix) * math.log(length) + mix * math.log(30.0)))


def tapped(before, block, taps):
    rows = block.shape[0]
    joined = jnp.concatenate([before, block], axis=0)
    total = taps[0:1] * block
    for lag in range(1, SHORT):
        total = total + taps[lag : lag + 1] * joined[HALO - lag : HALO - lag + rows]
    return total


def keep_mask(bits):
    bits = bits ^ lax.shift_right_logical(bits, jnp.full_like(bits, 16))
    bits = bits * jnp.int32(2146121005)
    bits = bits ^ lax.shift_right_logical(bits, jnp.full_like(bits, 15))
    bits = bits * jnp.int32(-2073254261)
    bits = bits ^ lax.shift_right_logical(bits, jnp.full_like(bits, 16))
    return lax.shift_right_logical(bits, jnp.full_like(bits, 29)) != 0


def spread(table, row, lanes):
    return jnp.broadcast_to(table[row : row + 1, lanes], (CHUNKS, LANES))


def gate_kernel(length, step, unroll, base_ref, feat_ref, edge_ref, taps_ref, mix_ref,
                gated_ref, start_ref, end_ref, wide, sums):
    rows, width = gated_ref.shape
    groups = width // LANES
    modes = mix_ref.shape[0]
    parts = start_ref.shape[1] // (modes * CHUNKS)
    run_len = rows // (CHUNKS * parts)
    first_channel = pl.program_id(0) * width
    base = base_ref[0] + first_channel * jnp.int32(CHAN_MULT)
    shape = (step, width)
    offsets = (
        lax.broadcasted_iota(jnp.int32, shape, 0) * jnp.int32(POS_MULT)
        + lax.broadcasted_iota(jnp.int32, shape, 1) * jnp.int32(CHAN_MULT)
    )
    key_taps, value_taps = taps_ref[1], taps_ref[2]

    def gate(index, before):
        at = pl.ds(pl.multiple_of(index * step, step), step)
        key_in = feat_ref[1, at, :].astype(jnp.float32)
        value_in = feat_ref[2, at, :].astype(jnp.float32)
        keyed = tapped(before[0], key_in, key_taps)
        valued = tapped(before[1], value_in, value_taps)
        bits = offsets + (base + index * step * jnp.int32(POS_MULT))
        gated = jnp.where(keep_mask(bits), keyed * valued * keep_scale, 0.0).astype(jnp.bfloat16)
        gated_ref[at, :] = gated
        full = gated.astype(jnp.float32)
        for group in range(groups):
            wide[group, at, :] = full[:, group * LANES : (group + 1) * LANES]
        return (key_in[step - HALO :], value_in[step - HALO :])

    lax.fori_loop(
        0, rows // step, gate,
        (edge_ref[1].astype(jnp.float32), edge_ref[2].astype(jnp.float32)),
    )

    rate = rates_of(mix_ref[...], length)
    decay = jnp.exp(-rate)
    decay_run = jnp.exp(-rate * run_len)
    for group in range(groups):
        lanes = slice(group * LANES, (group + 1) * LANES)
        factors = [spread(decay, mode, lanes) for mode in range(modes)]

        running = jnp.zeros((modes, LANES), jnp.float32)
        for part in range(parts):

            def advance(block, states):
                for inner in range(unroll):
                    first = part * CHUNKS * run_len + block * unroll + inner
                    x = wide[group, pl.ds(first, CHUNKS, stride=run_len), :]
                    states = tuple(f * s + x for f, s in zip(factors, states))
                return states

            states = lax.fori_loop(
                0, run_len // unroll, advance,
                tuple(jnp.zeros((CHUNKS, LANES), jnp.float32) for _ in range(modes)),
            )
            for mode in range(modes):
                sums[part, pl.ds(mode * CHUNKS, CHUNKS), :] = states[mode]
            for chunk in range(CHUNKS):
                start_ref[group, pl.ds((part * CHUNKS + chunk) * modes, modes), :] = running
                running = (
                    decay_run[:, lanes] * running
                    + sums[part, pl.ds(chunk, modes, stride=CHUNKS), :]
                )
        end_ref[:, lanes] = running


def part_at(index, tiles):
    count = lax.axis_size("ch")
    return lax.rem(lax.axis_index("ch") + 1 + index // tiles, count)


def conv_kernel(length, device_rows, lags, step, unroll, feat_ref, prior_ref, edge_ref, taps_ref,
                residue_ref, mix_ref, skip_ref, gated_ref, start_ref, *rest):
    end_refs, weight_ref, out_ref = rest[:lags], rest[lags], rest[lags + 1]
    (wide, inits, mixed_ref, weight, sending, arriving, load_sem, send_sem, recv_sem) = rest[lags + 2 :]
    index = pl.program_id(0)
    tiles = pl.num_programs(0) // 2
    other = 1 - lax.axis_index("ch")
    pieces, _, piece = sending.shape
    lane_start = pl.multiple_of(lax.rem(index, tiles) * gated_ref.shape[1], gated_ref.shape[1])

    def load(at):
        return pltpu.make_async_copy(
            weight_ref.at[:, pl.ds(pl.multiple_of(at * piece, piece), piece)],
            weight.at[at], load_sem.at[at],
        )

    def exchange(at):
        return pltpu.make_async_remote_copy(
            src_ref=sending.at[at], dst_ref=arriving.at[at],
            send_sem=send_sem.at[at], recv_sem=recv_sem.at[at],
            device_id={"ch": other}, device_id_type=pl.DeviceIdType.MESH,
        )

    @pl.when(index == 0)
    def _():
        barrier = pltpu.get_barrier_semaphore()
        pl.semaphore_signal(
            barrier, inc=1, device_id={"ch": other}, device_id_type=pl.DeviceIdType.MESH
        )
        pl.semaphore_wait(barrier, 1)

        def begin(at, carry):
            load(at).start()
            return carry

        lax.fori_loop(0, pieces, begin, 0)

    rows, width = gated_ref.shape
    groups = width // LANES
    modes = mix_ref.shape[0]
    run_len = rows // CHUNKS
    part = part_at(index, tiles)

    def widen(index, carry):
        at = pl.ds(pl.multiple_of(index * step, step), step)
        full = gated_ref[at, :].astype(jnp.float32)
        for group in range(groups):
            wide[group, at, :] = full[:, group * LANES : (group + 1) * LANES]
        return carry

    lax.fori_loop(0, rows // step, widen, 0)
    rate = rates_of(mix_ref[...], length)
    decay = jnp.exp(-rate)
    residue = residue_ref[...]
    entry = jnp.zeros_like(rate)
    for back, end_ref in enumerate(end_refs):
        entry = entry + jnp.exp(-rate * (device_rows * back)) * end_ref[...]
    for group in range(groups):
        lanes = slice(group * LANES, (group + 1) * LANES)
        for chunk in range(CHUNKS):
            at = pl.ds(chunk * modes, modes)
            reach = jnp.exp(-rate[:, lanes] * (part * rows + run_len * chunk).astype(jnp.float32))
            inits[at, :] = residue[:, lanes] * (start_ref[group, at, :] + reach * entry[:, lanes])
        factors = [spread(decay, mode, lanes) for mode in range(modes)]
        gains = [spread(residue, mode, lanes) for mode in range(modes)]

        def advance(block, states):
            for inner in range(unroll):
                at = pl.ds(block * unroll + inner, CHUNKS, stride=run_len)
                x = wide[group, at, :]
                states = tuple(f * s + k * x for f, s, k in zip(factors, states, gains))
                parts = list(states)
                while len(parts) > 1:
                    odd = [parts[-1]] if len(parts) % 2 else []
                    parts = [p + q for p, q in zip(parts[0::2], parts[1::2])] + odd
                wide[group, at, :] = parts[0]
            return states

        lax.fori_loop(
            0, run_len // unroll, advance,
            tuple(inits[pl.ds(mode, CHUNKS, stride=modes), :] for mode in range(modes)),
        )

    taps = taps_ref[0]
    skip = skip_ref[...]

    def mix(index, before):
        at = pl.ds(pl.multiple_of(index * step, step), step)
        query_in = feat_ref[0, at, :].astype(jnp.float32)
        query = tapped(before, query_in, taps)
        convolved = jnp.concatenate([wide[group, at, :] for group in range(groups)], axis=1)
        long_out = convolved + skip * gated_ref[at, :].astype(jnp.float32)
        mixed_ref[at, pl.ds(lane_start, width)] = (query * long_out).astype(jnp.bfloat16)
        return query_in[step - HALO :]

    before = jnp.where(
        part == 0,
        edge_ref[0].astype(jnp.float32),
        prior_ref[0].astype(jnp.float32)[prior_ref.shape[1] - HALO :],
    )
    lax.fori_loop(0, rows // step, mix, before)

    @pl.when(index == tiles - 1)
    def _():
        def send(at, carry):
            load(at).wait()
            part_sum = jnp.dot(mixed_ref[...], weight[at], preferred_element_type=jnp.float32)
            sending[at] = part_sum.astype(jnp.bfloat16)
            exchange(at).start()
            return carry

        lax.fori_loop(0, pieces, send, 0)

    @pl.when(index == 2 * tiles - 1)
    def _():
        def finish(at, carry):
            own = jnp.dot(mixed_ref[...], weight[at], preferred_element_type=jnp.float32)
            exchange(at).wait()
            cut = pl.ds(pl.multiple_of(at * piece, piece), piece)
            out_ref[:, cut] = (own + arriving[at].astype(jnp.float32)).astype(jnp.bfloat16)
            return carry

        lax.fori_loop(0, pieces, finish, 0)


def body(features, short_filter, mode_residue, decay_mix, skip_gain, counter, out_weight):
    rows, kinds, width = features.shape
    modes = mode_residue.shape[0]
    ctx_count = lax.axis_size("ctx")
    ch_count = lax.axis_size("ch")
    length = rows * ctx_count
    half = rows // ch_count
    run_len = half // CHUNKS
    tile = 2 * LANES if width % (2 * LANES) == 0 else LANES
    groups = tile // LANES
    step = min(64, half)
    unroll = min(8, run_len)
    grid = (width // tile,)
    prior = 2 * HALO

    planes = features.transpose(1, 0, 2)
    edge = passed_along(planes[:, rows - HALO :], "ctx", 1)
    first = counter[1] + lax.axis_index("ctx") * rows
    base = (
        counter[0] + first * jnp.int32(POS_MULT)
        + lax.axis_index("ch") * width * jnp.int32(CHAN_MULT)
    )[None]

    params = pltpu.CompilerParams(vmem_limit_bytes=60 * 1024 * 1024)

    gated, starts, ends = pl.pallas_call(
        functools.partial(gate_kernel, length, step, unroll),
        grid=grid,
        in_specs=[
            pl.BlockSpec(memory_space=pltpu.SMEM),
            pl.BlockSpec((kinds, rows, tile), lambda i: (0, 0, i)),
            pl.BlockSpec((kinds, HALO, tile), lambda i: (0, 0, i)),
            pl.BlockSpec((kinds, SHORT, tile), lambda i: (0, 0, i)),
            pl.BlockSpec((modes, tile), lambda i: (0, i)),
        ],
        out_specs=[
            pl.BlockSpec((rows, tile), lambda i: (0, i)),
            pl.BlockSpec((groups, ch_count * modes * CHUNKS, LANES), lambda i: (i, 0, 0)),
            pl.BlockSpec((modes, tile), lambda i: (0, i)),
        ],
        out_shape=[
            jax.ShapeDtypeStruct((rows, width), jnp.bfloat16),
            jax.ShapeDtypeStruct((width // LANES, ch_count * modes * CHUNKS, LANES), jnp.float32),
            jax.ShapeDtypeStruct((modes, width), jnp.float32),
        ],
        scratch_shapes=[
            pltpu.VMEM((groups, rows, LANES), jnp.float32),
            pltpu.VMEM((ch_count, modes * CHUNKS, LANES), jnp.float32),
        ],
        compiler_params=params,
        cost_estimate=pl.CostEstimate(flops=10**10, bytes_accessed=10**7, transcendentals=0),
        name="gate",
    )(base, planes, edge, short_filter, decay_mix)

    arrived = [passed_along(ends, "ctx", steps) for steps in range(1, ctx_count)]
    tiles = grid[0]
    pieces = 8
    piece = out_weight.shape[1] // pieces
    mode_block = pl.BlockSpec((modes, tile), lambda i: (0, lax.rem(i, tiles)))

    return pl.pallas_call(
        functools.partial(conv_kernel, length, rows, len(arrived), step, unroll),
        grid=(2 * tiles,),
        in_specs=[
            pl.BlockSpec((1, half, tile), lambda i: (0, part_at(i, tiles), lax.rem(i, tiles))),
            pl.BlockSpec(
                (1, prior, tile),
                lambda i: (
                    0,
                    jnp.maximum(part_at(i, tiles) * (half // prior) - 1, 0),
                    lax.rem(i, tiles),
                ),
            ),
            pl.BlockSpec((1, HALO, tile), lambda i: (0, 0, lax.rem(i, tiles))),
            pl.BlockSpec((kinds, SHORT, tile), lambda i: (0, 0, lax.rem(i, tiles))),
            mode_block,
            mode_block,
            pl.BlockSpec((1, tile), lambda i: (0, lax.rem(i, tiles))),
            pl.BlockSpec((half, tile), lambda i: (part_at(i, tiles), lax.rem(i, tiles))),
            pl.BlockSpec(
                (groups, modes * CHUNKS, LANES),
                lambda i: (lax.rem(i, tiles), part_at(i, tiles), 0),
            ),
        ] + [mode_block] * len(arrived) + [pl.BlockSpec(memory_space=pl.ANY)],
        out_specs=pl.BlockSpec((half, out_weight.shape[1]), lambda i: (0, 0)),
        scratch_shapes=[
            pltpu.VMEM((groups, half, LANES), jnp.float32),
            pltpu.VMEM((modes * CHUNKS, LANES), jnp.float32),
            pltpu.VMEM((half, width), jnp.bfloat16),
            pltpu.VMEM((pieces, width, piece), jnp.bfloat16),
            pltpu.VMEM((pieces, half, piece), jnp.bfloat16),
            pltpu.VMEM((pieces, half, piece), jnp.bfloat16),
            pltpu.SemaphoreType.DMA((pieces,)),
            pltpu.SemaphoreType.DMA((pieces,)),
            pltpu.SemaphoreType.DMA((pieces,)),
        ],
        out_shape=jax.ShapeDtypeStruct((half, out_weight.shape[1]), jnp.bfloat16),
        compiler_params=pltpu.CompilerParams(
            vmem_limit_bytes=60 * 1024 * 1024, collective_id=0, has_side_effects=True
        ),
        name="conv_project",
    )(
        planes, planes, edge, short_filter, mode_residue, decay_mix, skip_gain[None], gated,
        starts, *arrived, out_weight,
    )


def solution(mesh):
    placed = (
        P(("dp", "ctx"), None, "ch"),
        P(None, None, "ch"),
        P(None, "ch"),
        P(None, "ch"),
        P("ch"),
        P("dp"),
        P("ch", None),
    )
    return jax.shard_map(
        body, mesh=mesh, in_specs=placed, out_specs=P(("dp", "ctx", "ch"), None), check_vma=False
    )
```

```python
import functools
import math

import jax
import jax.numpy as jnp
from jax import lax
from jax.experimental import pallas as pl
from jax.experimental.pallas import tpu as pltpu
from jax.sharding import PartitionSpec as P

SHORT = 3
LANES = 128
CHUNKS = 8
HALO = 8
keep_scale = 8.0 / 7.0
POS_MULT = -1640531535
CHAN_MULT = -2048144777


def passed_along(value, axis, steps):
    count = lax.axis_size(axis)
    return lax.ppermute(value, axis, [(source, source + steps) for source in range(count - steps)])


def rates_of(mix, length):
    return jnp.exp(-((1.0 - mix) * math.log(length) + mix * math.log(30.0)))


def tapped(before, block, taps):
    rows = block.shape[0]
    joined = jnp.concatenate([before, block], axis=0)
    total = taps[0:1] * block
    for lag in range(1, SHORT):
        total = total + taps[lag : lag + 1] * joined[HALO - lag : HALO - lag + rows]
    return total


def keep_mask(bits):
    bits = bits ^ lax.shift_right_logical(bits, jnp.full_like(bits, 16))
    bits = bits * jnp.int32(2146121005)
    bits = bits ^ lax.shift_right_logical(bits, jnp.full_like(bits, 15))
    bits = bits * jnp.int32(-2073254261)
    bits = bits ^ lax.shift_right_logical(bits, jnp.full_like(bits, 16))
    return lax.shift_right_logical(bits, jnp.full_like(bits, 29)) != 0


def spread(table, row, lanes):
    return jnp.broadcast_to(table[row : row + 1, lanes], (CHUNKS, LANES))


def gate_kernel(length, step, unroll, base_ref, feat_ref, edge_ref, taps_ref, mix_ref,
                gated_ref, start_ref, end_ref, wide, sums):
    rows, width = gated_ref.shape
    groups = width // LANES
    modes = mix_ref.shape[0]
    parts = start_ref.shape[1] // (modes * CHUNKS)
    run_len = rows // (CHUNKS * parts)
    first_channel = pl.program_id(0) * width
    base = base_ref[0] + first_channel * jnp.int32(CHAN_MULT)
    shape = (step, width)
    offsets = (
        lax.broadcasted_iota(jnp.int32, shape, 0) * jnp.int32(POS_MULT)
        + lax.broadcasted_iota(jnp.int32, shape, 1) * jnp.int32(CHAN_MULT)
    )
    key_taps, value_taps = taps_ref[1], taps_ref[2]

    def gate(index, before):
        at = pl.ds(pl.multiple_of(index * step, step), step)
        key_in = feat_ref[1, at, :].astype(jnp.float32)
        value_in = feat_ref[2, at, :].astype(jnp.float32)
        keyed = tapped(before[0], key_in, key_taps)
        valued = tapped(before[1], value_in, value_taps)
        bits = offsets + (base + index * step * jnp.int32(POS_MULT))
        gated = jnp.where(keep_mask(bits), keyed * valued * keep_scale, 0.0).astype(jnp.bfloat16)
        gated_ref[at, :] = gated
        full = gated.astype(jnp.float32)
        for group in range(groups):
            wide[group, at, :] = full[:, group * LANES : (group + 1) * LANES]
        return (key_in[step - HALO :], value_in[step - HALO :])

    lax.fori_loop(
        0, rows // step, gate,
        (edge_ref[1].astype(jnp.float32), edge_ref[2].astype(jnp.float32)),
    )

    rate = rates_of(mix_ref[...], length)
    decay = jnp.exp(-rate)
    decay_run = jnp.exp(-rate * run_len)
    for group in range(groups):
        lanes = slice(group * LANES, (group + 1) * LANES)
        factors = [spread(decay, mode, lanes) for mode in range(modes)]

        running = jnp.zeros((modes, LANES), jnp.float32)
        for part in range(parts):

            def advance(block, states):
                for inner in range(unroll):
                    first = part * CHUNKS * run_len + block * unroll + inner
                    x = wide[group, pl.ds(first, CHUNKS, stride=run_len), :]
                    states = tuple(f * s + x for f, s in zip(factors, states))
                return states

            states = lax.fori_loop(
                0, run_len // unroll, advance,
                tuple(jnp.zeros((CHUNKS, LANES), jnp.float32) for _ in range(modes)),
            )
            for mode in range(modes):
                sums[part, pl.ds(mode * CHUNKS, CHUNKS), :] = states[mode]
            for chunk in range(CHUNKS):
                start_ref[group, pl.ds((part * CHUNKS + chunk) * modes, modes), :] = running
                running = (
                    decay_run[:, lanes] * running
                    + sums[part, pl.ds(chunk, modes, stride=CHUNKS), :]
                )
        end_ref[:, lanes] = running


def part_at(index, tiles):
    count = lax.axis_size("ch")
    return lax.rem(lax.axis_index("ch") + 1 + index // tiles, count)


def conv_kernel(length, device_rows, step, unroll, feat_ref, prior_ref, edge_ref, taps_ref,
                residue_ref, mix_ref, skip_ref, gated_ref, start_ref, ends_ref, weight_ref,
                out_ref, wide, inits, mixed_ref, weight, sending, arriving, states_in,
                load_sem, send_sem, recv_sem, state_send_sem, state_recv_sem):
    index = pl.program_id(0)
    tiles = pl.num_programs(0) // 2
    other = 1 - lax.axis_index("ch")
    here = lax.axis_index("ctx")
    lags = states_in.shape[0]
    pieces, _, piece = sending.shape
    lane_start = pl.multiple_of(lax.rem(index, tiles) * gated_ref.shape[1], gated_ref.shape[1])

    def load(at):
        return pltpu.make_async_copy(
            weight_ref.at[:, pl.ds(pl.multiple_of(at * piece, piece), piece)],
            weight.at[at], load_sem.at[at],
        )

    def exchange(at):
        return pltpu.make_async_remote_copy(
            src_ref=sending.at[at], dst_ref=arriving.at[at],
            send_sem=send_sem.at[at], recv_sem=recv_sem.at[at],
            device_id={"ch": other}, device_id_type=pl.DeviceIdType.MESH,
        )

    def later(lag):
        return lax.rem(here + lag + 1, lags + 1)

    def pass_states(lag):
        return pltpu.make_async_remote_copy(
            src_ref=ends_ref, dst_ref=states_in.at[lag],
            send_sem=state_send_sem.at[lag], recv_sem=state_recv_sem.at[lag],
            device_id={"ctx": later(lag)}, device_id_type=pl.DeviceIdType.MESH,
        )

    @pl.when(index == 0)
    def _():
        barrier = pltpu.get_barrier_semaphore()
        pl.semaphore_signal(
            barrier, inc=1, device_id={"ch": other}, device_id_type=pl.DeviceIdType.MESH
        )

        def greet(lag, carry):
            pl.semaphore_signal(
                barrier, inc=1, device_id={"ctx": later(lag)},
                device_id_type=pl.DeviceIdType.MESH,
            )
            return carry

        lax.fori_loop(0, lags, greet, 0)
        pl.semaphore_wait(barrier, lags + 1)

        def give(lag, carry):
            pass_states(lag).start()
            return carry

        lax.fori_loop(0, lags, give, 0)

        def begin(at, carry):
            load(at).start()
            return carry

        lax.fori_loop(0, pieces, begin, 0)

        def take(lag, carry):
            pass_states(lag).wait()
            return carry

        lax.fori_loop(0, lags, take, 0)

    rows, width = gated_ref.shape
    groups = width // LANES
    modes = mix_ref.shape[0]
    run_len = rows // CHUNKS
    part = part_at(index, tiles)

    def widen(index, carry):
        at = pl.ds(pl.multiple_of(index * step, step), step)
        full = gated_ref[at, :].astype(jnp.float32)
        for group in range(groups):
            wide[group, at, :] = full[:, group * LANES : (group + 1) * LANES]
        return carry

    lax.fori_loop(0, rows // step, widen, 0)
    rate = rates_of(mix_ref[...], length)
    decay = jnp.exp(-rate)
    residue = residue_ref[...]
    entry = jnp.zeros_like(rate)
    for back in range(lags):
        earlier = states_in[back, :, pl.ds(lane_start, width)]
        earlier = jnp.where(here > back, earlier, 0.0)
        entry = entry + jnp.exp(-rate * (device_rows * back)) * earlier
    for group in range(groups):
        lanes = slice(group * LANES, (group + 1) * LANES)
        for chunk in range(CHUNKS):
            at = pl.ds(chunk * modes, modes)
            reach = jnp.exp(-rate[:, lanes] * (part * rows + run_len * chunk).astype(jnp.float32))
            inits[at, :] = residue[:, lanes] * (start_ref[group, at, :] + reach * entry[:, lanes])
        factors = [spread(decay, mode, lanes) for mode in range(modes)]
        gains = [spread(residue, mode, lanes) for mode in range(modes)]

        def advance(block, states):
            for inner in range(unroll):
                at = pl.ds(block * unroll + inner, CHUNKS, stride=run_len)
                x = wide[group, at, :]
                states = tuple(f * s + k * x for f, s, k in zip(factors, states, gains))
                parts = list(states)
                while len(parts) > 1:
                    odd = [parts[-1]] if len(parts) % 2 else []
                    parts = [p + q for p, q in zip(parts[0::2], parts[1::2])] + odd
                wide[group, at, :] = parts[0]
            return states

        lax.fori_loop(
            0, run_len // unroll, advance,
            tuple(inits[pl.ds(mode, CHUNKS, stride=modes), :] for mode in range(modes)),
        )

    taps = taps_ref[0]
    skip = skip_ref[...]

    def mix(index, before):
        at = pl.ds(pl.multiple_of(index * step, step), step)
        query_in = feat_ref[0, at, :].astype(jnp.float32)
        query = tapped(before, query_in, taps)
        convolved = jnp.concatenate([wide[group, at, :] for group in range(groups)], axis=1)
        long_out = convolved + skip * gated_ref[at, :].astype(jnp.float32)
        mixed_ref[at, pl.ds(lane_start, width)] = (query * long_out).astype(jnp.bfloat16)
        return query_in[step - HALO :]

    before = jnp.where(
        part == 0,
        edge_ref[0].astype(jnp.float32),
        prior_ref[0].astype(jnp.float32)[prior_ref.shape[1] - HALO :],
    )
    lax.fori_loop(0, rows // step, mix, before)

    @pl.when(index == tiles - 1)
    def _():
        def send(at, carry):
            load(at).wait()
            part_sum = jnp.dot(mixed_ref[...], weight[at], preferred_element_type=jnp.float32)
            sending[at] = part_sum.astype(jnp.bfloat16)
            exchange(at).start()
            return carry

        lax.fori_loop(0, pieces, send, 0)

    @pl.when(index == 2 * tiles - 1)
    def _():
        def finish(at, carry):
            own = jnp.dot(mixed_ref[...], weight[at], preferred_element_type=jnp.float32)
            exchange(at).wait()
            cut = pl.ds(pl.multiple_of(at * piece, piece), piece)
            out_ref[:, cut] = (own + arriving[at].astype(jnp.float32)).astype(jnp.bfloat16)
            return carry

        lax.fori_loop(0, pieces, finish, 0)


def body(features, short_filter, mode_residue, decay_mix, skip_gain, counter, out_weight):
    rows, kinds, width = features.shape
    modes = mode_residue.shape[0]
    ctx_count = lax.axis_size("ctx")
    ch_count = lax.axis_size("ch")
    length = rows * ctx_count
    half = rows // ch_count
    run_len = half // CHUNKS
    tile = 2 * LANES if width % (2 * LANES) == 0 else LANES
    groups = tile // LANES
    step = min(64, half)
    unroll = min(8, run_len)
    grid = (width // tile,)
    prior = 2 * HALO

    planes = features.transpose(1, 0, 2)
    edge = passed_along(planes[:, rows - HALO :], "ctx", 1)
    first = counter[1] + lax.axis_index("ctx") * rows
    base = (
        counter[0] + first * jnp.int32(POS_MULT)
        + lax.axis_index("ch") * width * jnp.int32(CHAN_MULT)
    )[None]

    params = pltpu.CompilerParams(vmem_limit_bytes=60 * 1024 * 1024)

    gated, starts, ends = pl.pallas_call(
        functools.partial(gate_kernel, length, step, unroll),
        grid=grid,
        in_specs=[
            pl.BlockSpec(memory_space=pltpu.SMEM),
            pl.BlockSpec((kinds, rows, tile), lambda i: (0, 0, i)),
            pl.BlockSpec((kinds, HALO, tile), lambda i: (0, 0, i)),
            pl.BlockSpec((kinds, SHORT, tile), lambda i: (0, 0, i)),
            pl.BlockSpec((modes, tile), lambda i: (0, i)),
        ],
        out_specs=[
            pl.BlockSpec((rows, tile), lambda i: (0, i)),
            pl.BlockSpec((groups, ch_count * modes * CHUNKS, LANES), lambda i: (i, 0, 0)),
            pl.BlockSpec((modes, tile), lambda i: (0, i)),
        ],
        out_shape=[
            jax.ShapeDtypeStruct((rows, width), jnp.bfloat16),
            jax.ShapeDtypeStruct((width // LANES, ch_count * modes * CHUNKS, LANES), jnp.float32),
            jax.ShapeDtypeStruct((modes, width), jnp.float32),
        ],
        scratch_shapes=[
            pltpu.VMEM((groups, rows, LANES), jnp.float32),
            pltpu.VMEM((ch_count, modes * CHUNKS, LANES), jnp.float32),
        ],
        compiler_params=params,
        cost_estimate=pl.CostEstimate(flops=10**10, bytes_accessed=10**7, transcendentals=0),
        name="gate",
    )(base, planes, edge, short_filter, decay_mix)

    tiles = grid[0]
    pieces = 8
    piece = out_weight.shape[1] // pieces
    mode_block = pl.BlockSpec((modes, tile), lambda i: (0, lax.rem(i, tiles)))

    return pl.pallas_call(
        functools.partial(conv_kernel, length, rows, step, unroll),
        grid=(2 * tiles,),
        in_specs=[
            pl.BlockSpec((1, half, tile), lambda i: (0, part_at(i, tiles), lax.rem(i, tiles))),
            pl.BlockSpec(
                (1, prior, tile),
                lambda i: (
                    0,
                    jnp.maximum(part_at(i, tiles) * (half // prior) - 1, 0),
                    lax.rem(i, tiles),
                ),
            ),
            pl.BlockSpec((1, HALO, tile), lambda i: (0, 0, lax.rem(i, tiles))),
            pl.BlockSpec((kinds, SHORT, tile), lambda i: (0, 0, lax.rem(i, tiles))),
            mode_block,
            mode_block,
            pl.BlockSpec((1, tile), lambda i: (0, lax.rem(i, tiles))),
            pl.BlockSpec((half, tile), lambda i: (part_at(i, tiles), lax.rem(i, tiles))),
            pl.BlockSpec(
                (groups, modes * CHUNKS, LANES),
                lambda i: (lax.rem(i, tiles), part_at(i, tiles), 0),
            ),
        ] + [pl.BlockSpec(memory_space=pl.ANY)] * 2,
        out_specs=pl.BlockSpec((half, out_weight.shape[1]), lambda i: (0, 0)),
        scratch_shapes=[
            pltpu.VMEM((groups, half, LANES), jnp.float32),
            pltpu.VMEM((modes * CHUNKS, LANES), jnp.float32),
            pltpu.VMEM((half, width), jnp.bfloat16),
            pltpu.VMEM((pieces, width, piece), jnp.bfloat16),
            pltpu.VMEM((pieces, half, piece), jnp.bfloat16),
            pltpu.VMEM((pieces, half, piece), jnp.bfloat16),
            pltpu.VMEM((ctx_count - 1, modes, width), jnp.float32),
            pltpu.SemaphoreType.DMA((pieces,)),
            pltpu.SemaphoreType.DMA((pieces,)),
            pltpu.SemaphoreType.DMA((pieces,)),
            pltpu.SemaphoreType.DMA((ctx_count - 1,)),
            pltpu.SemaphoreType.DMA((ctx_count - 1,)),
        ],
        out_shape=jax.ShapeDtypeStruct((half, out_weight.shape[1]), jnp.bfloat16),
        compiler_params=pltpu.CompilerParams(
            vmem_limit_bytes=60 * 1024 * 1024, collective_id=0, has_side_effects=True
        ),
        name="conv_project",
    )(
        planes, planes, edge, short_filter, mode_residue, decay_mix, skip_gain[None], gated,
        starts, ends, out_weight,
    )


def solution(mesh):
    placed = (
        P(("dp", "ctx"), None, "ch"),
        P(None, None, "ch"),
        P(None, "ch"),
        P(None, "ch"),
        P("ch"),
        P("dp"),
        P("ch", None),
    )
    return jax.shard_map(
        body, mesh=mesh, in_specs=placed, out_specs=P(("dp", "ctx", "ch"), None), check_vma=False
    )
```
